512 devices in a mesh: row: 32 (over y, x, core), col: 16 (over z).
Axes of the slice: x: 4, y: 4, z: 16, core: 2. Of those that a mesh axis runs over, the one named last changes fastest.
Arguments:
- left_factors: bfloat16 [2, 32, 2, 16, 512, 128], P(None, 'row', None, 'col'), may hold values from -6 to 6
- right_factors: bfloat16 [2, 32, 2, 16, 512, 128], P(None, 'row', None, 'col'), may hold values from -0.5 to 0.5
- ranks: int32 [2, 32, 2, 16], P(None, 'row', None, 'col'), may hold values from 32 to 128, as said below
- pivot_inverses: bfloat16 [2, 512, 512], replicated, may hold values from -0.0048828125 to 0.0048828125
Outputs:
- factored: bfloat16 [2, 32, 2, 16, 512, 512], P(None, 'row', None, 'col')
The draws below stay inside these ranges and needn't reach their ends.
Inputs may be any that keep to these rules, and one draw needn't show every extreme that they name: `ranks`: every rank is a multiple of 16.
All inputs are finite; a program needn't handle non-finite values.
Results may differ from the reference program's by a relative error of at most 0.0054.
Values may be sent and summed in bfloat16 or wider, within the bound.
No kernel may reach another device: no remote copies, remote signals or barrier semaphores. Data moves between devices by JAX's collectives and lax.ppermute only.
A program may use at most 64 MiB of HBM per device.

```python
import jax
import jax.numpy as jnp
from jax import lax

B = 512
R = 128
TR_DEV = 2
TC_DEV = 2
N_ROW = 32
N_COL = 16


def draw_ranks(key, part):
    key = jax.random.fold_in(key, 11)
    values = 16 * jax.random.randint(key, (TR_DEV, N_ROW, TC_DEV, N_COL), 2, 9)
    values = values.at[0, 0, 0, 0].set(128).at[0, 1, 0, 0].set(32)
    return values.astype(jnp.int32)


def level_of(rng, extent, pieces, least, top_value):
    def one(position, blocks):
        steps = jax.random.uniform(jax.random.fold_in(jax.random.fold_in(rng, 6), position), (blocks,), jnp.float32, least / len(pieces), top_value / len(pieces))
        return jnp.repeat(jnp.exp(steps), extent[position] // blocks).reshape((-1,) + (1,) * (len(extent) - position - 1))

    loudness = one(*pieces[0])
    for cut in pieces[1:]:
        loudness = loudness * one(*cut)
    return loudness


def gaussian(rng, dims, scale, most, cuts=(), kind=jnp.bfloat16):
    values = jax.random.normal(rng, dims, jnp.float32) * scale
    if len(cuts) > 0:
        values = level_of(rng, dims, cuts, -0.22, 0.18) * values
    return jnp.clip(values, min=-most, max=most).astype(kind)


def setup_inputs(seed: int = 0) -> dict:
    seeds = jax.random.split(jax.random.key(seed), 5)
    left_factors = gaussian(seeds[0], (TR_DEV, N_ROW, TC_DEV, N_COL, B, R), 1.0, 6.0, ((1, 32), (3, 16)))
    right_factors = gaussian(seeds[1], (TR_DEV, N_ROW, TC_DEV, N_COL, B, R), R ** -0.5, 0.5, ((1, 32), (3, 16)))
    ranks = draw_ranks(jax.random.fold_in(seeds[4], 71), 0)
    pivot_inverses = gaussian(seeds[3], (2, B, B), (6 * B * B) ** -0.5, 0.0048828125)
    return dict(left_factors=left_factors, right_factors=right_factors, ranks=ranks, pivot_inverses=pivot_inverses)


def product(form, first, second):
    return jnp.einsum(form, first.astype(jnp.float32), second.astype(jnp.float32))


def reference(left_factors, right_factors, ranks, pivot_inverses):
    tile_rows = TR_DEV * N_ROW
    tile_cols = TC_DEV * N_COL
    left_tiles = left_factors.reshape(tile_rows, tile_cols, B, R)
    right_tiles = right_factors.reshape(tile_rows, tile_cols, B, R)
    rank_grid = ranks.reshape(tile_rows, tile_cols)
    rank_keep = jnp.arange(R, dtype=jnp.int32)[None, None, None, :] < rank_grid[:, :, None, None]
    left_tiles = jnp.where(rank_keep, left_tiles, 0.0).astype(jnp.bfloat16)
    right_tiles = jnp.where(rank_keep, right_tiles, 0.0).astype(jnp.bfloat16)
    inverse_one = pivot_inverses[0]
    inverse_two = pivot_inverses[1]
    row_ids = jnp.arange(tile_rows, dtype=jnp.int32)
    col_ids = jnp.arange(tile_cols, dtype=jnp.int32)
    lower_first = product('kn,ikr->inr', inverse_one, right_tiles[:, 0]).astype(jnp.bfloat16)
    up_left = left_tiles[0]
    up_right = right_tiles[0]
    middle_col = product('inr,ns->irs', lower_first, up_left[1])
    middle_col = jnp.where((row_ids > 0)[:, None, None], middle_col, 0.0).astype(jnp.bfloat16)
    update_col = product('inr,irs->ins', left_tiles[:, 0], middle_col).astype(jnp.bfloat16)
    middle_row = product('nr,jns->jrs', lower_first[1], up_left)
    middle_row = jnp.where((col_ids > 0)[:, None, None], middle_row, 0.0).astype(jnp.bfloat16)
    update_row = product('nr,jrs->jns', left_tiles[1, 0], middle_row).astype(jnp.bfloat16)
    fresh_right = product('kn,ikr->inr', inverse_two, right_tiles[:, 1]).astype(jnp.bfloat16)
    pivot_right = product('kn,kr->nr', inverse_two, right_tiles[0, 1]).astype(jnp.bfloat16)
    second_left = jnp.concatenate([left_tiles[:, 1], -update_col], axis=-1)
    second_right = jnp.concatenate([fresh_right, jnp.broadcast_to(pivot_right[None], fresh_right.shape)], axis=-1)
    upper_left = jnp.concatenate([left_tiles[1], -update_row], axis=-1)
    upper_right = jnp.concatenate([right_tiles[1], right_tiles[0]], axis=-1)

    def tile_row(index):
        middle_one = product('nr,jns->jrs', lower_first[index], up_left)
        middle_one = jnp.where(((index > 0) & (col_ids > 0))[:, None, None], middle_one, 0.0).astype(jnp.bfloat16)
        update_one = product('nr,jrs->jns', left_tiles[index, 0], middle_one).astype(jnp.bfloat16)
        middle_two = product('nr,jns->jrs', second_right[index], upper_left)
        middle_two = jnp.where(((index > 1) & (col_ids > 1))[:, None, None], middle_two, 0.0).astype(jnp.bfloat16)
        update_two = product('nr,jrs->jns', second_left[index], middle_two).astype(jnp.bfloat16)
        is_first = ((col_ids == 0) & (index > 0))[:, None, None]
        is_second = ((col_ids == 1) & (index > 1))[:, None, None]
        first_block = jnp.where(is_first, lower_first[index][None], jnp.where(is_second, fresh_right[index][None], right_tiles[index]))
        second_block = jnp.where(is_second, pivot_right[None], up_right)
        all_left = jnp.concatenate([left_tiles[index], -update_one, -update_two], axis=-1)
        all_right = jnp.concatenate([first_block, second_block, upper_right], axis=-1)
        return product('jnr,jmr->jnm', all_left, all_right).astype(jnp.bfloat16)

    result = lax.map(tile_row, row_ids)
    return result.reshape(TR_DEV, N_ROW, TC_DEV, N_COL, B, B)
```

```python
import jax
import jax.numpy as jnp
from jax import lax
from jax.sharding import PartitionSpec as P

AG_ROWS = 104
TREE_ROWS = 384
N_COL = 16
N_ROW = 32


def transform(inverse, factors):
    return jnp.einsum(
        "kn,...kr->...nr", inverse, factors, preferred_element_type=jnp.float32
    ).astype(jnp.bfloat16)


def pick(conditions, values):
    out = values[-1]
    for condition, value in zip(reversed(conditions), reversed(values[:-1])):
        out = jnp.where(condition, value, out)
    return out


def column_pieces(panel):
    q = lax.axis_index("col")
    tree = panel[:TREE_ROWS]
    pieces = panel[TREE_ROWS:].reshape(N_COL, AG_ROWS, 128)

    def group(a):
        members = [(4 * a - 1 + m) % N_COL for m in range(4)]
        return jnp.concatenate([tree] + [pieces[m] for m in members], axis=0)

    groups = [group(a) for a in range(4)]
    near = lax.ppermute(jnp.where(q == 0, groups[1], groups[3]), "col", [(0, 4), (1, 13)])
    back = lax.ppermute(jnp.where(q == 0, groups[3], groups[1]), "col", [(0, 12), (1, 5)])
    far = lax.ppermute(groups[2], "col", [(0, 8), (1, 9)])
    return groups[0], near, back, far


def spread(own, near, back, far):
    q = lax.axis_index("col")
    head = pick(
        [q < 2, (q == 4) | (q == 13), (q == 12) | (q == 5)], [own, near, back, far]
    )
    tree = head[:TREE_ROWS]
    part = [head[TREE_ROWS + AG_ROWS * m : TREE_ROWS + AG_ROWS * (m + 1)] for m in range(4)]
    even = q % 4 == 0

    def message(first, second):
        return jnp.concatenate([tree, jnp.where(even, part[first], part[second])], axis=0)

    starts = range(0, N_COL, 4)
    one = lax.ppermute(
        message(2, 1), "col", [(s, s + 1) for s in starts] + [(s + 1, s) for s in starts]
    )
    two = lax.ppermute(
        message(3, 0),
        "col",
        [(s, s + 2) for s in starts] + [(s + 1, (s - 1) % N_COL) for s in starts],
    )
    three = lax.ppermute(
        message(0, 3),
        "col",
        [(s, (s - 1) % N_COL) for s in starts] + [(s + 1, s + 2) for s in starts],
    )
    kept = message(1, 2)
    which = q % 4
    order = [which == 0, which == 1, which == 2]
    first = pick(order, [kept, one, two, three])
    second = pick(order, [one, kept, three, two])
    return first, second


def per_device(left_factors, right_factors, ranks, pivot_inverses):
    shape_four = (2, 2, 512, 128)
    p = lax.axis_index("row")
    q = lax.axis_index("col")
    row_ids = jnp.arange(2, dtype=jnp.int32) * N_ROW + p
    col_ids = jnp.arange(2, dtype=jnp.int32) * N_COL + q
    rank_grid = ranks.reshape(2, 2)
    rank_keep = jnp.arange(128, dtype=jnp.int32)[None, None, None, :] < rank_grid[:, :, None, None]
    left_tiles = jnp.where(rank_keep, left_factors.reshape(shape_four), 0.0)
    right_tiles = jnp.where(rank_keep, right_factors.reshape(shape_four), 0.0)
    inverse_one = pivot_inverses[0]
    inverse_two = pivot_inverses[1]

    panel = jnp.concatenate([left_tiles[:, 0], right_tiles[:, 0]], axis=0).reshape(2048, 128)
    own, near, back, far = column_pieces(panel)

    top = jnp.concatenate([left_tiles[0], right_tiles[0]], axis=0).reshape(4, N_ROW, 16, 128)
    top = top.transpose(1, 0, 2, 3)
    scattered = lax.all_to_all(top, "row", 0, 0, tiled=True)[:2]

    first, second = spread(own, near, back, far)
    corner = jnp.where(q == 0, scattered[1], scattered[0])
    corner = jnp.concatenate([corner[0], corner[2]], axis=0)

    rows_all = lax.all_gather(scattered.reshape(128, 128), "row").reshape(N_ROW, 2, 4, 16, 128)
    rows_all = rows_all.transpose(1, 2, 0, 3, 4).reshape(2, 2, 2, 512, 128)
    up_left, up_right = rows_all[0, 0], rows_all[0, 1]
    low_left, low_right = rows_all[1, 0], rows_all[1, 1]

    gathered = lax.all_gather(
        jnp.concatenate([first[TREE_ROWS:], second[TREE_ROWS:], corner], axis=0), "col"
    )
    corner = jnp.concatenate([gathered[0, 2 * AG_ROWS :], gathered[1, 2 * AG_ROWS :]], axis=0)
    corner = lax.all_to_all(
        jnp.broadcast_to(corner[None], (N_ROW, 64, 128)), "row", 0, 0, tiled=True
    )
    corner = corner.reshape(N_ROW, 4, 16, 128).transpose(1, 0, 2, 3).reshape(4, 512, 128)
    left_ten, right_ten, left_one, right_one = corner[0], corner[1], corner[2], corner[3]

    def assemble(tree, pieces):
        return jnp.concatenate(
            [tree[:TREE_ROWS], pieces.reshape(N_COL * AG_ROWS, 128)], axis=0
        ).reshape(2, 2, 512, 128)

    panel_one = assemble(first, gathered[:, :AG_ROWS])
    panel_two = assemble(second, gathered[:, AG_ROWS : 2 * AG_ROWS])
    got_left, col_left = panel_one[0], panel_two[0]
    got_right = transform(inverse_one, panel_one[1])
    fresh = transform(inverse_two, panel_two[1])
    pivot = transform(inverse_two, right_one)
    lower_ten = transform(inverse_one, right_ten)

    def middle(lower, upper, form, keep):
        product = jnp.einsum(form, lower, upper, preferred_element_type=jnp.float32)
        return jnp.where(keep, product, 0.0).astype(jnp.bfloat16)

    def apply(left, inner, form):
        return jnp.einsum(form, left, inner, preferred_element_type=jnp.float32).astype(
            jnp.bfloat16
        )

    mask_one = ((row_ids[:, None] > 0) & (col_ids[None, :] > 0))[:, :, None, None]
    middle_one = middle(got_right, up_left, "anr,bns->abrs", mask_one)
    update_one = apply(got_left, middle_one, "anr,abrs->abns")
    middle_col = middle(got_right, left_one, "anr,ns->ars", (row_ids > 0)[:, None, None])
    update_col = apply(got_left, middle_col, "anr,ars->ans")
    middle_row = middle(lower_ten, up_left, "nr,bns->brs", (col_ids > 0)[:, None, None])
    update_row = apply(left_ten, middle_row, "nr,brs->bns")

    second_left = jnp.concatenate([col_left, -update_col], axis=-1)
    second_right = jnp.concatenate([fresh, jnp.broadcast_to(pivot[None], fresh.shape)], axis=-1)
    upper_left = jnp.concatenate([low_left, -update_row], axis=-1)
    upper_right = jnp.concatenate([low_right, up_right], axis=-1)
    mask_two = ((row_ids[:, None] > 1) & (col_ids[None, :] > 1))[:, :, None, None]
    middle_two = middle(second_right, upper_left, "anr,bns->abrs", mask_two)
    update_two = apply(second_left, middle_two, "anr,abrs->abns")

    is_first = ((col_ids[None, :] == 0) & (row_ids[:, None] > 0))[:, :, None, None]
    is_second = ((col_ids[None, :] == 1) & (row_ids[:, None] > 1))[:, :, None, None]
    first_block = jnp.where(
        is_first, got_right[:, None], jnp.where(is_second, fresh[:, None], right_tiles)
    )
    second_block = jnp.where(is_second, pivot[None, None], up_right[None])
    upper_block = jnp.broadcast_to(upper_right[None], (2, 2, 512, 256))
    all_left = jnp.concatenate([left_tiles, -update_one, -update_two], axis=-1)
    all_right = jnp.concatenate([first_block, second_block, upper_block], axis=-1)
    dense = jnp.einsum(
        "abnr,abmr->abnm", all_left, all_right, preferred_element_type=jnp.float32
    ).astype(jnp.bfloat16)
    return dense.reshape(2, 1, 2, 1, 512, 512)


def solution(mesh):
    in_specs = (
        P(None, "row", None, "col", None, None),
        P(None, "row", None, "col", None, None),
        P(None, "row", None, "col"),
        P(),
    )
    out_specs = P(None, "row", None, "col", None, None)
    return jax.shard_map(
        per_device, mesh=mesh, in_specs=in_specs, out_specs=out_specs, check_vma=False
    )
```

```python
import jax
import jax.numpy as jnp
from jax import lax
from jax.experimental import pallas as pl
from jax.experimental.pallas import tpu as pltpu
from jax.sharding import PartitionSpec as P

N_COL = 16
N_ROW = 32
PIECE = 256
MAIN = 240
REST = PIECE - MAIN
VMEM = pl.BlockSpec(memory_space=pltpu.VMEM)
SMEM = pl.BlockSpec(memory_space=pltpu.SMEM)
BF16 = jnp.bfloat16


def params():
    return pltpu.CompilerParams(vmem_limit_bytes=40 * 1024 * 1024)


def tn(first, second):
    return lax.dot_general(
        first, second, (((0,), (0,)), ((), ())), preferred_element_type=jnp.float32
    )


def nn(first, second):
    return jnp.dot(first, second, preferred_element_type=jnp.float32)


def nt(first, second):
    return lax.dot_general(
        first, second, (((1,), (1,)), ((), ())), preferred_element_type=jnp.float32
    )


def keep_if(condition, value):
    return jnp.where(condition, value, jnp.zeros_like(value))


def prepare_body(place, ranks, left, right, left_out, right_out, own, near, back, far, top):
    column = lax.broadcasted_iota(jnp.int32, (512, 128), 1)
    for a in range(2):
        for b in range(2):
            keep = column < ranks[2 * a + b]
            left_out[a, b] = jnp.where(keep, left[a, b], jnp.zeros_like(left[a, b]))
            right_out[a, b] = jnp.where(keep, right[a, b], jnp.zeros_like(right[a, b]))
    at_zero = place[1] == 0
    left_one, right_one = left_out[1, 0], right_out[1, 0]
    own[:512] = left_out[0, 0]
    near[:512] = jnp.where(at_zero, left_one, right_one)
    back[:512] = jnp.where(at_zero, right_one, left_one)
    far[:512] = right_out[0, 0]
    for k in range(8):
        tile = (left_out if k < 4 else right_out)[k // 2 % 2, 0]
        rest = tile[PIECE * (k % 2) + MAIN : PIECE * (k % 2 + 1)]
        for message in (own, near, back, far):
            message[512 + REST * k : 512 + REST * (k + 1)] = rest
    for b in range(2):
        top[:, b] = left_out[0, b].reshape(N_ROW, 16, 128)
        top[:, 2 + b] = right_out[0, b].reshape(N_ROW, 16, 128)


def prepare(place, ranks, left, right):
    message = jax.ShapeDtypeStruct((512 + 8 * REST, 128), BF16)
    four = jax.ShapeDtypeStruct((2, 2, 512, 128), BF16)
    return pl.pallas_call(
        prepare_body,
        out_shape=(four, four, message, message, message, message,
                   jax.ShapeDtypeStruct((N_ROW, 4, 16, 128), BF16)),
        in_specs=[SMEM, SMEM, VMEM, VMEM],
        out_specs=[VMEM] * 7,
        compiler_params=params(),
        cost_estimate=pl.CostEstimate(flops=10**6, bytes_accessed=3 * 2**20, transcendentals=0),
        name="prepare",
    )(place, ranks, left, right)


def update_body(
    place, left, right, main, mine, other, rows, inverses, out,
    got_left, got_lower, tall, second, update, wide, upper,
):
    p, q = place[0], place[1]
    step = pl.program_id(0)
    a, b = step // 2, step % 2

    def row_tile(t):
        return rows[:, t].reshape(512, 128)

    @pl.when(step == 0)
    def _():
        even = q % 2 == 0
        rests = (
            jnp.where(even, mine[...], other[...]),
            jnp.where(even, other[...], mine[...]),
        )

        def column_tile(panel, tile):
            parts = []
            for k in (2 * tile, 2 * tile + 1):
                parts += [main[2 * k + panel], rests[panel][REST * k : REST * (k + 1)]]
            return jnp.concatenate(parts, axis=0)

        left_ten, right_ten, left_one, right_one = [row_tile(8 + k) for k in range(4)]
        pivot = tn(inverses[1], right_one).astype(BF16)
        lower_ten = tn(inverses[0], right_ten).astype(BF16)
        for k in range(2):
            got_left[k] = column_tile(0, k)
            got_lower[k] = tn(inverses[0], column_tile(0, 2 + k)).astype(BF16)
            tall[k, :, :128] = column_tile(1, k)
            second[k, :, :128] = tn(inverses[1], column_tile(1, 2 + k)).astype(BF16)
            second[k, :, 128:] = pivot
            middle = keep_if((k > 0) | (p > 0), tn(got_lower[k], left_one)).astype(BF16)
            tall[k, :, 128:] = -nn(got_left[k], middle).astype(BF16)
            middle = keep_if((k > 0) | (q > 0), tn(lower_ten, row_tile(k))).astype(BF16)
            wide[k, :, :128] = row_tile(4 + k)
            wide[k, :, 128:] = -nn(left_ten, middle).astype(BF16)
            upper[k, :, :128] = row_tile(6 + k)
            upper[k, :, 128:] = row_tile(2 + k)
        for i in range(2):
            for j in range(2):
                keep = ((i > 0) | (p > 0)) & ((j > 0) | (q > 0))
                middle = keep_if(keep, tn(got_lower[i], row_tile(j))).astype(BF16)
                update[i, j] = -nn(got_left[i], middle).astype(BF16)

    row = a * N_ROW + p
    col = b * N_COL + q
    middle = keep_if((row > 1) & (col > 1), tn(second[a], wide[b])).astype(BF16)
    change = -nn(tall[a], middle).astype(BF16)
    is_first = (col == 0) & (row > 0)
    is_second = (col == 1) & (row > 1)
    near = jnp.where(
        is_first, got_lower[a], jnp.where(is_second, second[a, :, :128], right[a, b])
    )
    beside = jnp.where(is_second, second[a, :, 128:], upper[b, :, 128:])
    all_left = jnp.concatenate([left[a, b], update[a, b], change], axis=1)
    all_right = jnp.concatenate([near, beside, upper[b]], axis=1)
    out[0] = nt(all_left, all_right).astype(BF16)


def update_tiles(place, left, right, main, mine, other, rows, inverses):
    pair, double = (2, 512, 128), (2, 512, 256)
    return pl.pallas_call(
        update_body,
        grid=(4,),
        out_shape=jax.ShapeDtypeStruct((4, 512, 512), BF16),
        in_specs=[SMEM] + [VMEM] * 7,
        out_specs=pl.BlockSpec((1, 512, 512), lambda s: (s, 0, 0)),
        scratch_shapes=[
            pltpu.VMEM(shape, BF16)
            for shape in (pair, pair, double, double, (2, 2, 512, 128), double, double)
        ],
        compiler_params=params(),
        cost_estimate=pl.CostEstimate(
            flops=25 * 10**8, bytes_accessed=8 * 2**20, transcendentals=0
        ),
        name="update_tiles",
    )(place, left, right, main, mine, other, rows, inverses)


def to_all(block, axis, size):
    sent = jnp.broadcast_to(block[None], (size,) + block.shape)
    return lax.all_to_all(sent, axis, 0, 0, tiled=True)


def per_device(left_factors, right_factors, ranks, pivot_inverses):
    shape_four = (2, 2, 512, 128)
    p = lax.axis_index("row")
    q = lax.axis_index("col")
    place = jnp.stack([p, q]).astype(jnp.int32)
    left, right, own, near, back, far, top = prepare(
        place, ranks.reshape(4), left_factors.reshape(shape_four), right_factors.reshape(shape_four)
    )
    scattered = lax.all_to_all(top, "row", 0, 0, tiled=True)[:2]
    near = lax.ppermute(near, "col", [(0, 4), (1, 13)])
    back = lax.ppermute(back, "col", [(0, 12), (1, 5)])
    far = lax.ppermute(far, "col", [(0, 8), (1, 9)])

    corner = jnp.where(q == 0, scattered[1], scattered[0])
    corner = to_all(jnp.concatenate([corner[0], corner[2]], axis=0), "col", N_COL)
    corner = corner.reshape(N_COL, 32, 128)[:2].reshape(64, 128)

    head = jnp.where(
        q < 2,
        own,
        jnp.where((q == 4) | (q == 13), near, jnp.where((q == 12) | (q == 5), back, far)),
    )
    moved = lax.ppermute(
        head[PIECE:], "col", [(s + c, s + c + 2) for s in range(0, N_COL, 4) for c in range(2)]
    )
    kept = q % 4 < 2
    piece = jnp.where(kept, head[:MAIN], moved[:MAIN])
    mine = jnp.where(kept, head[512:], moved[PIECE:])
    other = lax.ppermute(mine, "col", [(i, i ^ 1) for i in range(N_COL)])

    block = jnp.concatenate([scattered.reshape(128, 128), corner], axis=0)
    block, piece = lax.optimization_barrier((block, piece))
    rows = to_all(block, "row", N_ROW).reshape(N_ROW, 12, 16, 128)
    main = lax.all_gather(piece, "col")
    dense = update_tiles(place, left, right, main, mine, other, rows, pivot_inverses)
    return dense.reshape(2, 1, 2, 1, 512, 512)


def solution(mesh):
    in_specs = (
        P(None, "row", None, "col", None, None),
        P(None, "row", None, "col", None, None),
        P(None, "row", None, "col"),
        P(),
    )
    out_specs = P(None, "row", None, "col", None, None)
    return jax.shard_map(
        per_device, mesh=mesh, in_specs=in_specs, out_specs=out_specs, check_vma=False
    )
```

```python
import jax
import jax.numpy as jnp
from jax import lax
from jax.experimental import pallas as pl
from jax.experimental.pallas import tpu as pltpu
from jax.sharding import PartitionSpec as P

N_COL = 16
N_ROW = 32
PIECE = 256
MAIN = 240
REST = PIECE - MAIN
HOLDERS = ((0, 14, 2, 4, 6, 8, 12, 10), (1, 3, 5, 7, 11, 9, 15, 13))
VMEM = pl.BlockSpec(memory_space=pltpu.VMEM)
SMEM = pl.BlockSpec(memory_space=pltpu.SMEM)
HBM = pl.BlockSpec(memory_space=pltpu.HBM)
BF16 = jnp.bfloat16


def params():
    return pltpu.CompilerParams(vmem_limit_bytes=24 * 1024 * 1024)


def cost(flops, size):
    return pl.CostEstimate(flops=flops, bytes_accessed=size, transcendentals=0)


def tn(first, second):
    return lax.dot_general(
        first, second, (((0,), (0,)), ((), ())), preferred_element_type=jnp.float32
    )


def nn(first, second):
    return jnp.dot(first, second, preferred_element_type=jnp.float32)


def nt(first, second):
    return lax.dot_general(
        first, second, (((1,), (1,)), ((), ())), preferred_element_type=jnp.float32
    )


def mask_rank(tile, rank):
    column = lax.broadcasted_iota(jnp.int32, (512, 128), 1)
    return jnp.where(column < rank, tile, jnp.zeros_like(tile))


def in_hbm(*arrays):
    return [pltpu.with_memory_space_constraint(x, pltpu.HBM) for x in arrays]


def fetch(pairs, arrived):
    copies = [
        pltpu.make_async_copy(source, target, arrived.at[k])
        for k, (source, target) in enumerate(pairs)
    ]
    for copy in copies:
        copy.start()
    return copies


def top_body(ranks, left, right, top, left_row, right_row, arrived):
    pairs = ((left.at[0, 0, :, 0], left_row), (right.at[0, 0, :, 0], right_row))
    for k, copy in enumerate(fetch(pairs, arrived)):
        copy.wait()
        for b in range(2):
            tile = mask_rank(pairs[k][1][b], ranks[0, 0, 0, b])
            top[:, 2 * k + b] = tile.reshape(N_ROW, 16, 128)


def top_rows(ranks, left, right):
    return pl.pallas_call(
        top_body,
        out_shape=jax.ShapeDtypeStruct((N_ROW, 4, 16, 128), BF16),
        in_specs=[SMEM, HBM, HBM],
        out_specs=VMEM,
        scratch_shapes=[pltpu.VMEM((2, 512, 128), BF16)] * 2 + [pltpu.SemaphoreType.DMA((2,))],
        compiler_params=params(),
        cost_estimate=cost(10**6, 2**20),
        name="top_rows",
    )(ranks, *in_hbm(left, right))


def messages_body(
    place, ranks, left, right, own, near, middle, far, left_col, right_col, arrived
):
    pairs = ((left.at[:, 0, 0, 0], left_col), (right.at[:, 0, 0, 0], right_col))
    for copy in fetch(pairs, arrived):
        copy.wait()
    tiles = [mask_rank(ref[a], ranks[a, 0, 0, 0]) for ref in (left_col, right_col) for a in range(2)]
    at_zero = place[1] == 0
    own[:512] = tiles[0]
    near[:512] = jnp.where(at_zero, tiles[1], tiles[3])
    middle[:512] = jnp.where(at_zero, tiles[3], tiles[1])
    far[:512] = tiles[2]
    for k in range(8):
        rest = tiles[k // 2][PIECE * (k % 2) + MAIN : PIECE * (k % 2 + 1)]
        for message in (own, near, middle, far):
            message[512 + REST * k : 512 + REST * (k + 1)] = rest


def messages(place, ranks, left, right):
    message = jax.ShapeDtypeStruct((512 + 8 * REST, 128), BF16)
    return pl.pallas_call(
        messages_body,
        out_shape=(message,) * 4,
        in_specs=[SMEM, SMEM, HBM, HBM],
        out_specs=[VMEM] * 4,
        scratch_shapes=[pltpu.VMEM((2, 512, 128), BF16)] * 2 + [pltpu.SemaphoreType.DMA((2,))],
        compiler_params=params(),
        cost_estimate=cost(10**6, 2**20),
        name="messages",
    )(place, ranks, *in_hbm(left, right))


def update_body(
    place, ranks, left_hbm, right_hbm, main_hbm, inverses_hbm, mine, other, rows, out,
    left, right, main, inverses, arrived, lowers, ups, second, wide, tall, upper, update, change,
):
    p, q = place[0], place[1]
    step = pl.program_id(0)
    a, b = step // 2, step % 2

    def row_tile(t):
        return rows[:, t].reshape(512, 128)

    @pl.when(step == 0)
    def _():
        pairs = (
            (main_hbm, main),
            (inverses_hbm, inverses),
            (left_hbm.at[:, 0, :, 0], left),
            (right_hbm.at[:, 0, :, 0], right),
        )
        copies = fetch(pairs, arrived)
        copies[0].wait()
        copies[1].wait()
        even = q % 2 == 0
        rests = (
            jnp.where(even, mine[...], other[...]),
            jnp.where(even, other[...], mine[...]),
        )

        def column_tile(panel, tile):
            parts = []
            for k in (2 * tile, 2 * tile + 1):
                parts += [main[HOLDERS[panel][k]], rests[panel][REST * k : REST * (k + 1)]]
            return jnp.concatenate(parts, axis=0)

        raw = jnp.concatenate([column_tile(0, 2), column_tile(0, 3), row_tile(9)], axis=1)
        lowers[...] = tn(inverses[0], raw).astype(BF16)
        ups[...] = jnp.concatenate([row_tile(0), row_tile(1), row_tile(10)], axis=1)
        raw = jnp.concatenate([column_tile(1, 2), column_tile(1, 3), row_tile(11)], axis=1)
        fresh = tn(inverses[1], raw).astype(BF16)
        second[:, :128] = fresh[:, :128]
        second[:, 128:256] = fresh[:, 256:]
        second[:, 256:384] = fresh[:, 128:256]
        second[:, 384:] = fresh[:, 256:]

        line = lax.broadcasted_iota(jnp.int32, (384, 384), 0)
        column = lax.broadcasted_iota(jnp.int32, (384, 384), 1)
        drop = ((line < 128) & (p == 0)) | ((column < 128) & (q == 0))
        product = tn(lowers[...], ups[...])
        inner = jnp.where(drop, 0.0, product).astype(BF16)
        for k in range(2):
            result = -nn(column_tile(0, k), inner[128 * k : 128 * (k + 1)])
            update[k] = result.astype(BF16)
            tall[k, :, :128] = column_tile(1, k)
            tall[k, :, 128:] = update[k, :, 256:]
            upper[k, :, :128] = row_tile(6 + k)
            upper[k, :, 128:] = row_tile(2 + k)
        result = -nn(row_tile(8), inner[256:, :256])
        for k in range(2):
            wide[:, 256 * k : 256 * k + 128] = row_tile(4 + k)
            wide[:, 256 * k + 128 : 256 * k + 256] = result[:, 128 * k : 128 * (k + 1)].astype(BF16)

        line = lax.broadcasted_iota(jnp.int32, (512, 512), 0)
        column = lax.broadcasted_iota(jnp.int32, (512, 512), 1)
        drop = ((line < 256) & (p <= 1)) | ((column < 256) & (q <= 1))
        product = tn(second[...], wide[...])
        inner = jnp.where(drop, 0.0, product).astype(BF16)
        for k in range(2):
            result = -nn(tall[k], inner[256 * k : 256 * (k + 1)])
            for j in range(2):
                change[k, j] = result[:, 256 * j : 256 * (j + 1)].astype(BF16)
        copies[2].wait()
        copies[3].wait()

    row = a * N_ROW + p
    col = b * N_COL + q
    rank = ranks[a, 0, 0, b]
    is_first = (col == 0) & (row > 0)
    is_second = (col == 1) & (row > 1)

    def pick(ref, width):
        return jnp.where(a == 0, ref[:, :128], ref[:, width : width + 128])

    near = jnp.where(
        is_first,
        pick(lowers, 128),
        jnp.where(is_second, pick(second, 256), mask_rank(right[a, b], rank)),
    )
    beside = jnp.where(is_second, second[:, 128:256], upper[b, :, 128:])
    done = jnp.where(b == 0, update[a, :, :128], update[a, :, 128:256])
    all_left = jnp.concatenate([mask_rank(left[a, b], rank), done, change[a, b]], axis=1)
    all_right = jnp.concatenate([near, beside, upper[b]], axis=1)
    out[0, 0, 0, 0] = nt(all_left, all_right).astype(BF16)


def update_tiles(place, ranks, left, right, main, mine, other, rows, inverses):
    four = pltpu.VMEM((2, 2, 512, 128), BF16)
    shapes = (
        (512, 384), (512, 384), (512, 512), (512, 512),
        (2, 512, 256), (2, 512, 256), (2, 512, 384), (2, 2, 512, 256),
    )
    return pl.pallas_call(
        update_body,
        grid=(4,),
        out_shape=jax.ShapeDtypeStruct((2, 1, 2, 1, 512, 512), BF16),
        in_specs=[SMEM, SMEM] + [HBM] * 4 + [VMEM] * 3,
        out_specs=pl.BlockSpec(
            (1, 1, 1, 1, 512, 512), lambda s: (s // 2, 0, s % 2, 0, 0, 0)
        ),
        scratch_shapes=[four, four, pltpu.VMEM((N_COL, MAIN, 128), BF16)]
        + [pltpu.VMEM((2, 512, 512), BF16), pltpu.SemaphoreType.DMA((4,))]
        + [pltpu.VMEM(shape, BF16) for shape in shapes],
        compiler_params=params(),
        cost_estimate=cost(25 * 10**8, 8 * 2**20),
        name="update_tiles",
    )(place, ranks, *in_hbm(left, right, main, inverses), mine, other, rows)


def to_all(block, axis, size):
    sent = jnp.broadcast_to(block[None], (size,) + block.shape)
    return lax.all_to_all(sent, axis, 0, 0, tiled=True)


def per_device(left, right, ranks, pivot_inverses):
    p = lax.axis_index("row")
    q = lax.axis_index("col")
    place = jnp.stack([p, q]).astype(jnp.int32)
    ranks = ranks.reshape(2, 1, 1, 2)
    top = top_rows(ranks, left, right)
    own, near, middle, far = messages(place, ranks, left, right)
    near = lax.ppermute(near, "col", [(0, 2), (1, 15)])
    middle = lax.ppermute(middle, "col", [(0, 12), (1, 5)])
    far = lax.ppermute(far, "col", [(0, 6), (1, 11)])
    scattered = lax.all_to_all(top, "row", 0, 0, tiled=True)[:2]

    corner = jnp.where(q == 0, scattered[1], scattered[0])
    corner = to_all(jnp.concatenate([corner[0], corner[2]], axis=0), "col", N_COL)
    corner = corner.reshape(N_COL, 32, 128)[:2].reshape(64, 128)

    by_near = (q == 2) | (q == 15)
    by_middle = (q == 12) | (q == 5)
    is_head = (q < 2) | by_near | by_middle | (q == 6) | (q == 11)
    head = jnp.where(q < 2, own, jnp.where(by_near, near, jnp.where(by_middle, middle, far)))
    hops = [(line[k], line[k + 1]) for line in HOLDERS for k in range(0, 8, 2)]
    moved = lax.ppermute(head[PIECE:], "col", hops)
    piece = jnp.where(is_head, head[:MAIN], moved[:MAIN])
    mine = jnp.where(is_head, head[512:], moved[PIECE:])
    other = lax.ppermute(mine, "col", [(i, i ^ 1) for i in range(N_COL)])

    block = jnp.concatenate([scattered.reshape(128, 128), corner], axis=0)
    block, piece = lax.optimization_barrier((block, piece))
    rows = to_all(block, "row", N_ROW).reshape(N_ROW, 12, 16, 128)
    main = lax.all_gather(piece, "col")
    return update_tiles(place, ranks, left, right, main, mine, other, rows, pivot_inverses)


def solution(mesh):
    in_specs = (
        P(None, "row", None, "col", None, None),
        P(None, "row", None, "col", None, None),
        P(None, "row", None, "col"),
        P(),
    )
    out_specs = P(None, "row", None, "col", None, None)
    return jax.shard_map(
        per_device, mesh=mesh, in_specs=in_specs, out_specs=out_specs, check_vma=False
    )
```

```python
import jax
import jax.numpy as jnp
from jax import lax
from jax.experimental import pallas as pl
from jax.experimental.pallas import tpu as pltpu
from jax.sharding import PartitionSpec as P

N_COL = 16
N_ROW = 32
PIECE = 256
MAIN = 240
REST = PIECE - MAIN
HOLDERS = ((0, 14, 2, 4, 6, 8, 12, 10), (1, 3, 5, 7, 11, 9, 15, 13))
OTHER_ONE = ((0, 1), (2, 3), (6, 7), (12, 13), (1, 0), (5, 6), (11, 10), (15, 14))
OTHER_TWO = ((0, 15), (2, 5), (6, 9), (12, 11), (1, 2), (5, 4), (11, 8), (15, 12))
VMEM = pl.BlockSpec(memory_space=pltpu.VMEM)
SMEM = pl.BlockSpec(memory_space=pltpu.SMEM)
HBM = pl.BlockSpec(memory_space=pltpu.HBM)
BF16 = jnp.bfloat16


def params():
    return pltpu.CompilerParams(vmem_limit_bytes=24 * 1024 * 1024)


def cost(flops, size):
    return pl.CostEstimate(flops=flops, bytes_accessed=size, transcendentals=0)


def tn(first, second):
    return lax.dot_general(
        first, second, (((0,), (0,)), ((), ())), preferred_element_type=jnp.float32
    )


def nn(first, second):
    return jnp.dot(first, second, preferred_element_type=jnp.float32)


def nt(first, second):
    return lax.dot_general(
        first, second, (((1,), (1,)), ((), ())), preferred_element_type=jnp.float32
    )


def mask_rank(tile, rank):
    column = lax.broadcasted_iota(jnp.int32, (1, 128), 1)
    return tile * jnp.where(column < rank, 1.0, 0.0).astype(BF16)


def in_hbm(*arrays):
    return [pltpu.with_memory_space_constraint(x, pltpu.HBM) for x in arrays]


def fetch(pairs, arrived):
    copies = [
        pltpu.make_async_copy(source, target, arrived.at[k])
        for k, (source, target) in enumerate(pairs)
    ]
    for copy in copies:
        copy.start()
    return copies


def top_body(ranks_hbm, left, right, top, ranks, left_row, right_row, arrived):
    pairs = (
        (ranks_hbm, ranks),
        (left.at[0, 0, :, 0], left_row),
        (right.at[0, 0, :, 0], right_row),
    )
    copies = fetch(pairs, arrived)
    copies[0].wait()
    for k in range(2):
        copies[1 + k].wait()
        for b in range(2):
            tile = mask_rank(pairs[1 + k][1][b], ranks[0, 0, 0, b])
            top[:, 2 * k + b] = tile.reshape(N_ROW, 16, 128)


def top_rows(ranks, left, right):
    return pl.pallas_call(
        top_body,
        out_shape=jax.ShapeDtypeStruct((N_ROW, 4, 16, 128), BF16),
        in_specs=[HBM] * 3,
        out_specs=VMEM,
        scratch_shapes=[pltpu.SMEM((2, 1, 1, 2), jnp.int32)]
        + [pltpu.VMEM((2, 512, 128), BF16)] * 2
        + [pltpu.SemaphoreType.DMA((3,))],
        compiler_params=params(),
        cost_estimate=cost(10**6, 2**20),
        name="top_rows",
    )(*in_hbm(ranks, left, right))


def messages_body(
    place, ranks, left, right, own, near, middle, far, left_col, right_col, arrived
):
    pairs = ((left.at[:, 0, 0, 0], left_col), (right.at[:, 0, 0, 0], right_col))
    for copy in fetch(pairs, arrived):
        copy.wait()
    tiles = [mask_rank(ref[a], ranks[a, 0, 0, 0]) for ref in (left_col, right_col) for a in range(2)]
    at_zero = place[1] == 0
    chosen = (
        tiles[0],
        jnp.where(at_zero, tiles[1], tiles[3]),
        jnp.where(at_zero, tiles[3], tiles[1]),
        tiles[2],
    )
    for message, tile in zip((own, near, middle, far), chosen):
        message[:MAIN] = tile[:MAIN]
        message[MAIN : 2 * MAIN] = tile[PIECE : PIECE + MAIN]
        for k in range(8):
            rest = tiles[k // 2][PIECE * (k % 2) + MAIN : PIECE * (k % 2 + 1)]
            message[2 * MAIN + REST * k : 2 * MAIN + REST * (k + 1)] = rest


def messages(place, ranks, left, right):
    message = jax.ShapeDtypeStruct((2 * MAIN + 8 * REST, 128), BF16)
    return pl.pallas_call(
        messages_body,
        out_shape=(message,) * 4,
        in_specs=[SMEM, SMEM, HBM, HBM],
        out_specs=[VMEM] * 4,
        scratch_shapes=[pltpu.VMEM((2, 512, 128), BF16)] * 2 + [pltpu.SemaphoreType.DMA((2,))],
        compiler_params=params(),
        cost_estimate=cost(10**6, 2**20),
        name="messages",
    )(place, ranks, *in_hbm(left, right))


def update_body(
    place, ranks, left_hbm, right_hbm, main_hbm, inverses_hbm, mine, other, rows, out,
    left, right, main, inverses, arrived, lowers, ups, second, wide, tall, upper, update, change,
):
    p, q = place[0], place[1]
    step = pl.program_id(0)
    a, b = step // 2, step % 2

    def row_tile(t):
        return rows[:, t].reshape(512, 128)

    @pl.when(step == 0)
    def _():
        pairs = (
            (inverses_hbm, inverses),
            (main_hbm, main),
            (left_hbm.at[:, 0, :, 0], left),
            (right_hbm.at[:, 0, :, 0], right),
        )
        copies = fetch(pairs, arrived)
        copies[0].wait()
        lowers[:, 256:] = tn(inverses[0], row_tile(9)).astype(BF16)
        pivot = tn(inverses[1], row_tile(11)).astype(BF16)
        second[:, 128:256] = pivot
        second[:, 384:] = pivot
        ups[...] = jnp.concatenate([row_tile(0), row_tile(1), row_tile(10)], axis=1)
        copies[1].wait()
        even = q % 2 == 0
        rests = (
            jnp.where(even, mine[...], other[...]),
            jnp.where(even, other[...], mine[...]),
        )

        def column_tile(panel, tile):
            parts = []
            for k in (2 * tile, 2 * tile + 1):
                parts += [main[HOLDERS[panel][k]], rests[panel][REST * k : REST * (k + 1)]]
            return jnp.concatenate(parts, axis=0)

        raw = jnp.concatenate([column_tile(0, 2), column_tile(0, 3)], axis=1)
        lowers[:, :256] = tn(inverses[0], raw).astype(BF16)
        raw = jnp.concatenate([column_tile(1, 2), column_tile(1, 3)], axis=1)
        fresh = tn(inverses[1], raw).astype(BF16)
        second[:, :128] = fresh[:, :128]
        second[:, 256:384] = fresh[:, 128:]

        line = lax.broadcasted_iota(jnp.int32, (384, 384), 0)
        column = lax.broadcasted_iota(jnp.int32, (384, 384), 1)
        drop = ((line < 128) & (p == 0)) | ((column < 128) & (q == 0))
        product = tn(lowers[...], ups[...])
        inner = jnp.where(drop, 0.0, product).astype(BF16)
        for k in range(2):
            result = -nn(column_tile(0, k), inner[128 * k : 128 * (k + 1)])
            update[k] = result.astype(BF16)
            tall[k, :, :128] = column_tile(1, k)
            tall[k, :, 128:] = update[k, :, 256:]
            upper[k, :, :128] = row_tile(6 + k)
            upper[k, :, 128:] = row_tile(2 + k)
        result = -nn(row_tile(8), inner[256:, :256])
        for k in range(2):
            wide[:, 256 * k : 256 * k + 128] = row_tile(4 + k)
            wide[:, 256 * k + 128 : 256 * k + 256] = result[:, 128 * k : 128 * (k + 1)].astype(BF16)

        line = lax.broadcasted_iota(jnp.int32, (512, 512), 0)
        column = lax.broadcasted_iota(jnp.int32, (512, 512), 1)
        drop = ((line < 256) & (p <= 1)) | ((column < 256) & (q <= 1))
        product = tn(second[...], wide[...])
        inner = jnp.where(drop, 0.0, product).astype(BF16)
        for k in range(2):
            result = -nn(tall[k], inner[256 * k : 256 * (k + 1)])
            for j in range(2):
                change[k, j] = result[:, 256 * j : 256 * (j + 1)].astype(BF16)
        copies[2].wait()
        copies[3].wait()

    row = a * N_ROW + p
    col = b * N_COL + q
    rank = ranks[a, 0, 0, b]
    is_first = (col == 0) & (row > 0)
    is_second = (col == 1) & (row > 1)

    def pick(ref, width):
        return jnp.where(a == 0, ref[:, :128], ref[:, width : width + 128])

    near = jnp.where(
        is_first,
        pick(lowers, 128),
        jnp.where(is_second, pick(second, 256), mask_rank(right[a, b], rank)),
    )
    beside = jnp.where(is_second, second[:, 128:256], upper[b, :, 128:])
    done = jnp.where(b == 0, update[a, :, :128], update[a, :, 128:256])
    all_left = jnp.concatenate([mask_rank(left[a, b], rank), done, change[a, b]], axis=1)
    all_right = jnp.concatenate([near, beside, upper[b]], axis=1)
    out[0, 0, 0, 0] = nt(all_left, all_right).astype(BF16)


def update_tiles(place, ranks, left, right, main, mine, other, rows, inverses):
    four = pltpu.VMEM((2, 2, 512, 128), BF16)
    shapes = (
        (512, 384), (512, 384), (512, 512), (512, 512),
        (2, 512, 256), (2, 512, 256), (2, 512, 384), (2, 2, 512, 256),
    )
    return pl.pallas_call(
        update_body,
        grid=(4,),
        out_shape=jax.ShapeDtypeStruct((2, 1, 2, 1, 512, 512), BF16),
        in_specs=[SMEM, SMEM] + [HBM] * 4 + [VMEM] * 3,
        out_specs=pl.BlockSpec(
            (1, 1, 1, 1, 512, 512), lambda s: (s // 2, 0, s % 2, 0, 0, 0)
        ),
        scratch_shapes=[four, four, pltpu.VMEM((N_COL, MAIN, 128), BF16)]
        + [pltpu.VMEM((2, 512, 512), BF16), pltpu.SemaphoreType.DMA((4,))]
        + [pltpu.VMEM(shape, BF16) for shape in shapes],
        compiler_params=params(),
        cost_estimate=cost(25 * 10**8, 8 * 2**20),
        name="update_tiles",
    )(place, ranks, *in_hbm(left, right, main, inverses), mine, other, rows)


def to_all(block, axis, size):
    sent = jnp.broadcast_to(block[None], (size,) + block.shape)
    return lax.all_to_all(sent, axis, 0, 0, tiled=True)


def per_device(left, right, ranks, pivot_inverses):
    p = lax.axis_index("row")
    q = lax.axis_index("col")
    place = jnp.stack([p, q]).astype(jnp.int32)
    ranks = ranks.reshape(2, 1, 1, 2)
    top = top_rows(ranks, left, right)
    own, near, middle, far = messages(place, ranks, left, right)
    near = lax.ppermute(near, "col", [(0, 2), (1, 15)])
    middle = lax.ppermute(middle, "col", [(0, 12), (1, 5)])
    far = lax.ppermute(far, "col", [(0, 6), (1, 11)])
    scattered = lax.all_to_all(top, "row", 0, 0, tiled=True)[:2]

    corner = jnp.where(q == 0, scattered[1], scattered[0])
    corner = to_all(jnp.concatenate([corner[0], corner[2]], axis=0), "col", N_COL)
    corner = corner.reshape(N_COL, 32, 128)[:2].reshape(64, 128)

    by_near = (q == 2) | (q == 15)
    by_middle = (q == 12) | (q == 5)
    is_head = (q < 2) | by_near | by_middle | (q == 6) | (q == 11)
    head = jnp.where(q < 2, own, jnp.where(by_near, near, jnp.where(by_middle, middle, far)))
    hops = [(line[k], line[k + 1]) for line in HOLDERS for k in range(0, 8, 2)]
    moved = lax.ppermute(head[MAIN:], "col", hops)
    piece = jnp.where(is_head, head[:MAIN], moved[:MAIN])
    mine = jnp.where(is_head, head[2 * MAIN :], moved[MAIN:])
    other = lax.ppermute(mine, "col", [(i, i ^ 1) for i in range(N_COL)])

    block = jnp.concatenate([scattered.reshape(128, 128), corner], axis=0)
    block, piece = lax.optimization_barrier((block, piece))
    rows = to_all(block, "row", N_ROW).reshape(N_ROW, 12, 16, 128)
    main = lax.all_gather(piece, "col")
    return update_tiles(place, ranks, left, right, main, mine, other, rows, pivot_inverses)


def solution(mesh):
    in_specs = (
        P(None, "row", None, "col", None, None),
        P(None, "row", None, "col", None, None),
        P(None, "row", None, "col"),
        P(),
    )
    out_specs = P(None, "row", None, "col", None, None)
    return jax.shard_map(
        per_device, mesh=mesh, in_specs=in_specs, out_specs=out_specs, check_vma=False
    )
```

```python
import jax
import jax.numpy as jnp
from jax import lax
from jax.experimental import pallas as pl
from jax.experimental.pallas import tpu as pltpu
from jax.sharding import PartitionSpec as P

N_COL = 16
N_ROW = 32
PIECE = 256
MAIN = 240
REST = PIECE - MAIN
HOLDERS = ((0, 14, 2, 4, 6, 8, 12, 10), (1, 3, 5, 7, 11, 9, 15, 13))
OTHER_ONE = ((0, 1), (2, 3), (6, 7), (12, 13), (1, 0), (5, 6), (11, 10), (15, 14))
OTHER_TWO = ((0, 15), (2, 5), (6, 9), (12, 11), (1, 2), (5, 4), (11, 8), (15, 12))
VMEM = pl.BlockSpec(memory_space=pltpu.VMEM)
SMEM = pl.BlockSpec(memory_space=pltpu.SMEM)
HBM = pl.BlockSpec(memory_space=pltpu.HBM)
BF16 = jnp.bfloat16


def params():
    return pltpu.CompilerParams(vmem_limit_bytes=24 * 1024 * 1024)


def cost(flops, size):
    return pl.CostEstimate(flops=flops, bytes_accessed=size, transcendentals=0)


def tn(first, second):
    return lax.dot_general(
        first, second, (((0,), (0,)), ((), ())), preferred_element_type=jnp.float32
    )


def nn(first, second):
    return jnp.dot(first, second, preferred_element_type=jnp.float32)


def nt(first, second):
    return lax.dot_general(
        first, second, (((1,), (1,)), ((), ())), preferred_element_type=jnp.float32
    )


def mask_rank(tile, rank):
    column = lax.broadcasted_iota(jnp.int32, (1, 128), 1)
    return tile * jnp.where(column < rank, 1.0, 0.0).astype(BF16)


def in_hbm(*arrays):
    return [pltpu.with_memory_space_constraint(x, pltpu.HBM) for x in arrays]


def fetch(pairs, arrived):
    copies = [
        pltpu.make_async_copy(source, target, arrived.at[k])
        for k, (source, target) in enumerate(pairs)
    ]
    for copy in copies:
        copy.start()
    return copies


def top_body(ranks_hbm, left, right, top, ranks, tiles, arrived):
    pairs = [(ranks_hbm, ranks)]
    for t in range(4):
        source = (left, right)[t // 2]
        pairs.append((source.at[0, 0, t % 2, 0], tiles.at[t]))
    copies = fetch(pairs, arrived)
    copies[0].wait()
    for t in range(4):
        copies[1 + t].wait()
        top[:, t] = mask_rank(tiles[t], ranks[0, 0, 0, t % 2]).reshape(N_ROW, 16, 128)


def top_rows(ranks, left, right):
    return pl.pallas_call(
        top_body,
        out_shape=jax.ShapeDtypeStruct((N_ROW, 4, 16, 128), BF16),
        in_specs=[HBM] * 3,
        out_specs=VMEM,
        scratch_shapes=[pltpu.SMEM((2, 1, 1, 2), jnp.int32)]
        + [pltpu.VMEM((4, 512, 128), BF16), pltpu.SemaphoreType.DMA((5,))],
        compiler_params=params(),
        cost_estimate=cost(10**6, 2**20),
        name="top_rows",
    )(*in_hbm(ranks, left, right))


def messages_body(
    place, ranks, left, right, own, near, middle, far, left_col, right_col, arrived
):
    pairs = ((left.at[:, 0, 0, 0], left_col), (right.at[:, 0, 0, 0], right_col))
    for copy in fetch(pairs, arrived):
        copy.wait()
    tiles = [mask_rank(ref[a], ranks[a, 0, 0, 0]) for ref in (left_col, right_col) for a in range(2)]
    at_zero = place[1] == 0
    chosen = (
        tiles[0],
        jnp.where(at_zero, tiles[1], tiles[3]),
        jnp.where(at_zero, tiles[3], tiles[1]),
        tiles[2],
    )
    for message, tile in zip((own, near, middle, far), chosen):
        message[:MAIN] = tile[:MAIN]
        message[MAIN : 2 * MAIN] = tile[PIECE : PIECE + MAIN]
        for k in range(8):
            rest = tiles[k // 2][PIECE * (k % 2) + MAIN : PIECE * (k % 2 + 1)]
            message[2 * MAIN + REST * k : 2 * MAIN + REST * (k + 1)] = rest


def messages(place, ranks, left, right):
    message = jax.ShapeDtypeStruct((2 * MAIN + 8 * REST, 128), BF16)
    return pl.pallas_call(
        messages_body,
        out_shape=(message,) * 4,
        in_specs=[SMEM, SMEM, HBM, HBM],
        out_specs=[VMEM] * 4,
        scratch_shapes=[pltpu.VMEM((2, 512, 128), BF16)] * 2 + [pltpu.SemaphoreType.DMA((2,))],
        compiler_params=params(),
        cost_estimate=cost(10**6, 2**20),
        name="messages",
    )(place, ranks, *in_hbm(left, right))


def update_body(
    place, ranks, left_hbm, right_hbm, inverses_hbm, main, mine, other, rows, out,
    left, right, inverses, arrived, lowers, ups, second, wide, tall, upper, update, change,
):
    p, q = place[0], place[1]
    step = pl.program_id(0)
    a, b = step // 2, step % 2

    def row_tile(t):
        return rows[:, t].reshape(512, 128)

    @pl.when(step == 0)
    def _():
        pairs = (
            (inverses_hbm, inverses),
            (left_hbm.at[:, 0, :, 0], left),
            (right_hbm.at[:, 0, :, 0], right),
        )
        copies = fetch(pairs, arrived)
        ups[...] = jnp.concatenate([row_tile(0), row_tile(1), row_tile(10)], axis=1)
        for k in range(2):
            wide[:, 256 * k : 256 * k + 128] = row_tile(4 + k)
            upper[k, :, :128] = row_tile(6 + k)
            upper[k, :, 128:] = row_tile(2 + k)
        copies[0].wait()
        lowers[:, 256:] = tn(inverses[0], row_tile(9)).astype(BF16)
        pivot = tn(inverses[1], row_tile(11)).astype(BF16)
        second[:, 128:256] = pivot
        second[:, 384:] = pivot
        even = q % 2 == 0
        rests = (
            jnp.where(even, mine[...], other[...]),
            jnp.where(even, other[...], mine[...]),
        )

        def column_tile(panel, tile):
            parts = []
            for k in (2 * tile, 2 * tile + 1):
                parts += [main[HOLDERS[panel][k]], rests[panel][REST * k : REST * (k + 1)]]
            return jnp.concatenate(parts, axis=0)

        raw = jnp.concatenate([column_tile(0, 2), column_tile(0, 3)], axis=1)
        lowers[:, :256] = tn(inverses[0], raw).astype(BF16)
        raw = jnp.concatenate([column_tile(1, 2), column_tile(1, 3)], axis=1)
        fresh = tn(inverses[1], raw).astype(BF16)
        second[:, :128] = fresh[:, :128]
        second[:, 256:384] = fresh[:, 128:]

        line = lax.broadcasted_iota(jnp.int32, (384, 384), 0)
        column = lax.broadcasted_iota(jnp.int32, (384, 384), 1)
        drop = ((line < 128) & (p == 0)) | ((column < 128) & (q == 0))
        product = tn(lowers[...], ups[...])
        inner = jnp.where(drop, 0.0, product).astype(BF16)
        for k in range(2):
            result = -nn(column_tile(0, k), inner[128 * k : 128 * (k + 1)])
            update[k] = result.astype(BF16)
            tall[k, :, :128] = column_tile(1, k)
            tall[k, :, 128:] = update[k, :, 256:]
        result = -nn(row_tile(8), inner[256:, :256])
        for k in range(2):
            wide[:, 256 * k + 128 : 256 * k + 256] = result[:, 128 * k : 128 * (k + 1)].astype(BF16)

        line = lax.broadcasted_iota(jnp.int32, (512, 512), 0)
        column = lax.broadcasted_iota(jnp.int32, (512, 512), 1)
        drop = ((line < 256) & (p <= 1)) | ((column < 256) & (q <= 1))
        product = tn(second[...], wide[...])
        inner = jnp.where(drop, 0.0, product).astype(BF16)
        for k in range(2):
            result = -nn(tall[k], inner[256 * k : 256 * (k + 1)])
            for j in range(2):
                change[k, j] = result[:, 256 * j : 256 * (j + 1)].astype(BF16)
        copies[1].wait()
        copies[2].wait()

    row = a * N_ROW + p
    col = b * N_COL + q
    rank = ranks[a, 0, 0, b]
    is_first = (col == 0) & (row > 0)
    is_second = (col == 1) & (row > 1)

    def pick(ref, width):
        return jnp.where(a == 0, ref[:, :128], ref[:, width : width + 128])

    near = jnp.where(
        is_first,
        pick(lowers, 128),
        jnp.where(is_second, pick(second, 256), mask_rank(right[a, b], rank)),
    )
    beside = jnp.where(is_second, second[:, 128:256], upper[b, :, 128:])
    done = jnp.where(b == 0, update[a, :, :128], update[a, :, 128:256])
    all_left = jnp.concatenate([mask_rank(left[a, b], rank), done, change[a, b]], axis=1)
    all_right = jnp.concatenate([near, beside, upper[b]], axis=1)
    out[0, 0, 0, 0] = nt(all_left, all_right).astype(BF16)


def update_tiles(place, ranks, left, right, main, mine, other, rows, inverses):
    four = pltpu.VMEM((2, 2, 512, 128), BF16)
    shapes = (
        (512, 384), (512, 384), (512, 512), (512, 512),
        (2, 512, 256), (2, 512, 256), (2, 512, 384), (2, 2, 512, 256),
    )
    return pl.pallas_call(
        update_body,
        grid=(4,),
        out_shape=jax.ShapeDtypeStruct((2, 1, 2, 1, 512, 512), BF16),
        in_specs=[SMEM, SMEM] + [HBM] * 3 + [VMEM] * 4,
        out_specs=pl.BlockSpec(
            (1, 1, 1, 1, 512, 512), lambda s: (s // 2, 0, s % 2, 0, 0, 0)
        ),
        scratch_shapes=[four, four]
        + [pltpu.VMEM((2, 512, 512), BF16), pltpu.SemaphoreType.DMA((4,))]
        + [pltpu.VMEM(shape, BF16) for shape in shapes],
        compiler_params=params(),
        cost_estimate=cost(25 * 10**8, 8 * 2**20),
        name="update_tiles",
    )(place, ranks, *in_hbm(left, right, inverses), main, mine, other, rows)


def to_all(block, axis, size):
    sent = jnp.broadcast_to(block[None], (size,) + block.shape)
    return lax.all_to_all(sent, axis, 0, 0, tiled=True)


def per_device(left, right, ranks, pivot_inverses):
    p = lax.axis_index("row")
    q = lax.axis_index("col")
    place = jnp.stack([p, q]).astype(jnp.int32)
    ranks = ranks.reshape(2, 1, 1, 2)
    top = top_rows(ranks, left, right)
    own, near, middle, far = messages(place, ranks, left, right)
    near = lax.ppermute(near, "col", [(0, 2), (1, 15)])
    middle = lax.ppermute(middle, "col", [(0, 12), (1, 5)])
    far = lax.ppermute(far, "col", [(0, 6), (1, 11)])
    scattered = lax.all_to_all(top, "row", 0, 0, tiled=True)[:2]

    corner = jnp.where(q == 0, scattered[1], scattered[0])
    corner = to_all(jnp.concatenate([corner[0], corner[2]], axis=0), "col", N_COL)
    corner = corner.reshape(N_COL, 32, 128)[:2].reshape(64, 128)

    by_near = (q == 2) | (q == 15)
    by_middle = (q == 12) | (q == 5)
    is_head = (q < 2) | by_near | by_middle | (q == 6) | (q == 11)
    head = jnp.where(q < 2, own, jnp.where(by_near, near, jnp.where(by_middle, middle, far)))
    hops = [(line[k], line[k + 1]) for line in HOLDERS for k in range(0, 8, 2)]
    moved = lax.ppermute(head[MAIN:], "col", hops)
    piece = jnp.where(is_head, head[:MAIN], moved[:MAIN])
    mine = jnp.where(is_head, head[2 * MAIN :], moved[MAIN:])
    other = lax.ppermute(mine, "col", [(i, i ^ 1) for i in range(N_COL)])

    block = jnp.concatenate([scattered.reshape(128, 128), corner], axis=0)
    block, piece = lax.optimization_barrier((block, piece))
    rows = to_all(block, "row", N_ROW).reshape(N_ROW, 12, 16, 128)
    main = lax.all_gather(piece, "col")
    return update_tiles(place, ranks, left, right, main, mine, other, rows, pivot_inverses)


def solution(mesh):
    in_specs = (
        P(None, "row", None, "col", None, None),
        P(None, "row", None, "col", None, None),
        P(None, "row", None, "col"),
        P(),
    )
    out_specs = P(None, "row", None, "col", None, None)
    return jax.shard_map(
        per_device, mesh=mesh, in_specs=in_specs, out_specs=out_specs, check_vma=False
    )
```

```python
import jax
import jax.numpy as jnp
from jax import lax
from jax.experimental import pallas as pl
from jax.experimental.pallas import tpu as pltpu
from jax.sharding import PartitionSpec as P

N_COL = 16
N_ROW = 32
PIECE = 256
MAIN = 240
REST = PIECE - MAIN
HOLDERS = ((0, 14, 2, 4, 6, 8, 12, 10), (1, 3, 5, 7, 11, 9, 15, 13))
OTHER_ONE = ((0, 1), (2, 3), (6, 7), (12, 13), (1, 0), (5, 6), (11, 10), (15, 14))
OTHER_TWO = ((0, 15), (2, 5), (6, 9), (12, 11), (1, 2), (5, 4), (11, 8), (15, 12))
VMEM = pl.BlockSpec(memory_space=pltpu.VMEM)
SMEM = pl.BlockSpec(memory_space=pltpu.SMEM)
HBM = pl.BlockSpec(memory_space=pltpu.HBM)
BF16 = jnp.bfloat16


def params():
    return pltpu.CompilerParams(vmem_limit_bytes=24 * 1024 * 1024)


def cost(flops, size):
    return pl.CostEstimate(flops=flops, bytes_accessed=size, transcendentals=0)


def tn(first, second):
    return lax.dot_general(
        first, second, (((0,), (0,)), ((), ())), preferred_element_type=jnp.float32
    )


def nn(first, second):
    return jnp.dot(first, second, preferred_element_type=jnp.float32)


def nt(first, second):
    return lax.dot_general(
        first, second, (((1,), (1,)), ((), ())), preferred_element_type=jnp.float32
    )


def mask_rank(tile, rank):
    column = lax.broadcasted_iota(jnp.int32, (1, 128), 1)
    return tile * jnp.where(column < rank, 1.0, 0.0).astype(BF16)


def in_hbm(*arrays):
    return [pltpu.with_memory_space_constraint(x, pltpu.HBM) for x in arrays]


def fetch(pairs, arrived):
    copies = [
        pltpu.make_async_copy(source, target, arrived.at[k])
        for k, (source, target) in enumerate(pairs)
    ]
    for copy in copies:
        copy.start()
    return copies


def top_body(ranks_hbm, left, right, top, ranks, tiles, arrived):
    pairs = [(ranks_hbm, ranks)]
    for t in range(4):
        source = (left, right)[t // 2]
        pairs.append((source.at[0, 0, t % 2, 0], tiles.at[t]))
    copies = fetch(pairs, arrived)
    copies[0].wait()
    for t in range(4):
        copies[1 + t].wait()
        top[:, t] = mask_rank(tiles[t], ranks[0, 0, 0, t % 2]).reshape(N_ROW, 16, 128)


def top_rows(ranks, left, right):
    return pl.pallas_call(
        top_body,
        out_shape=jax.ShapeDtypeStruct((N_ROW, 4, 16, 128), BF16),
        in_specs=[HBM] * 3,
        out_specs=VMEM,
        scratch_shapes=[pltpu.SMEM((2, 1, 1, 2), jnp.int32)]
        + [pltpu.VMEM((4, 512, 128), BF16), pltpu.SemaphoreType.DMA((5,))],
        compiler_params=params(),
        cost_estimate=cost(10**6, 2**20),
        name="top_rows",
    )(*in_hbm(ranks, left, right))


def messages_body(
    place, ranks, left, right, own, near, middle, far, left_col, right_col, arrived
):
    pairs = ((left.at[:, 0, 0, 0], left_col), (right.at[:, 0, 0, 0], right_col))
    for copy in fetch(pairs, arrived):
        copy.wait()
    tiles = [mask_rank(ref[a], ranks[a, 0, 0, 0]) for ref in (left_col, right_col) for a in range(2)]
    at_zero = place[1] == 0
    chosen = (
        tiles[0],
        jnp.where(at_zero, tiles[1], tiles[3]),
        jnp.where(at_zero, tiles[3], tiles[1]),
        tiles[2],
    )
    for message, tile in zip((own, near, middle, far), chosen):
        message[:MAIN] = tile[:MAIN]
        message[MAIN : 2 * MAIN] = tile[PIECE : PIECE + MAIN]
        for k in range(8):
            rest = tiles[k // 2][PIECE * (k % 2) + MAIN : PIECE * (k % 2 + 1)]
            message[2 * MAIN + REST * k : 2 * MAIN + REST * (k + 1)] = rest


def messages(place, ranks, left, right):
    message = jax.ShapeDtypeStruct((2 * MAIN + 8 * REST, 128), BF16)
    return pl.pallas_call(
        messages_body,
        out_shape=(message,) * 4,
        in_specs=[SMEM, SMEM, HBM, HBM],
        out_specs=[VMEM] * 4,
        scratch_shapes=[pltpu.VMEM((2, 512, 128), BF16)] * 2 + [pltpu.SemaphoreType.DMA((2,))],
        compiler_params=params(),
        cost_estimate=cost(10**6, 2**20),
        name="messages",
    )(place, ranks, *in_hbm(left, right))


def update_body(
    place, ranks, left_hbm, right_hbm, inverses_hbm, main, mine, other, rows, out,
    left, right, inverses, arrived, lowers, ups, second, wide, tall, upper, update, change,
):
    p, q = place[0], place[1]
    step = pl.program_id(0)
    a, b = step // 2, step % 2

    def row_tile(t):
        return rows[:, t].reshape(512, 128)

    @pl.when(step == 0)
    def _():
        copies = [
            pltpu.make_async_copy(inverses_hbm.at[k], inverses.at[k], arrived.at[k])
            for k in range(2)
        ]
        tiles = [
            pltpu.make_async_copy(left_hbm.at[:, 0, :, 0], left, arrived.at[2]),
            pltpu.make_async_copy(right_hbm.at[:, 0, :, 0], right, arrived.at[3]),
        ]
        for copy in copies:
            copy.start()
        ups[...] = jnp.concatenate([row_tile(0), row_tile(1), row_tile(10)], axis=1)
        for k in range(2):
            wide[:, 256 * k : 256 * k + 128] = row_tile(4 + k)
            upper[k, :, :128] = row_tile(6 + k)
            upper[k, :, 128:] = row_tile(2 + k)
        copies[0].wait()
        lowers[:, 256:] = tn(inverses[0], row_tile(9)).astype(BF16)
        for copy in tiles:
            copy.start()
        copies[1].wait()
        pivot = tn(inverses[1], row_tile(11)).astype(BF16)
        second[:, 128:256] = pivot
        second[:, 384:] = pivot
        even = q % 2 == 0
        rests = (
            jnp.where(even, mine[...], other[...]),
            jnp.where(even, other[...], mine[...]),
        )

        def column_tile(panel, tile):
            parts = []
            for k in (2 * tile, 2 * tile + 1):
                parts += [main[HOLDERS[panel][k]], rests[panel][REST * k : REST * (k + 1)]]
            return jnp.concatenate(parts, axis=0)

        raw = jnp.concatenate([column_tile(0, 2), column_tile(0, 3)], axis=1)
        lowers[:, :256] = tn(inverses[0], raw).astype(BF16)
        raw = jnp.concatenate([column_tile(1, 2), column_tile(1, 3)], axis=1)
        fresh = tn(inverses[1], raw).astype(BF16)
        second[:, :128] = fresh[:, :128]
        second[:, 256:384] = fresh[:, 128:]

        line = lax.broadcasted_iota(jnp.int32, (384, 384), 0)
        column = lax.broadcasted_iota(jnp.int32, (384, 384), 1)
        drop = ((line < 128) & (p == 0)) | ((column < 128) & (q == 0))
        product = tn(lowers[...], ups[...])
        inner = jnp.where(drop, 0.0, product).astype(BF16)
        for k in range(2):
            result = -nn(column_tile(0, k), inner[128 * k : 128 * (k + 1)])
            update[k] = result.astype(BF16)
            tall[k, :, :128] = column_tile(1, k)
            tall[k, :, 128:] = update[k, :, 256:]
        result = -nn(row_tile(8), inner[256:, :256])
        for k in range(2):
            wide[:, 256 * k + 128 : 256 * k + 256] = result[:, 128 * k : 128 * (k + 1)].astype(BF16)

        line = lax.broadcasted_iota(jnp.int32, (512, 512), 0)
        column = lax.broadcasted_iota(jnp.int32, (512, 512), 1)
        drop = ((line < 256) & (p <= 1)) | ((column < 256) & (q <= 1))
        product = tn(second[...], wide[...])
        inner = jnp.where(drop, 0.0, product).astype(BF16)
        for k in range(2):
            result = -nn(tall[k], inner[256 * k : 256 * (k + 1)])
            for j in range(2):
                change[k, j] = result[:, 256 * j : 256 * (j + 1)].astype(BF16)
        for copy in tiles:
            copy.wait()

    row = a * N_ROW + p
    col = b * N_COL + q
    rank = ranks[a, 0, 0, b]
    is_first = (col == 0) & (row > 0)
    is_second = (col == 1) & (row > 1)

    def pick(ref, width):
        return jnp.where(a == 0, ref[:, :128], ref[:, width : width + 128])

    near = jnp.where(
        is_first,
        pick(lowers, 128),
        jnp.where(is_second, pick(second, 256), mask_rank(right[a, b], rank)),
    )
    beside = jnp.where(is_second, second[:, 128:256], upper[b, :, 128:])
    done = jnp.where(b == 0, update[a, :, :128], update[a, :, 128:256])
    all_left = jnp.concatenate([mask_rank(left[a, b], rank), done, change[a, b]], axis=1)
    all_right = jnp.concatenate([near, beside, upper[b]], axis=1)
    out[0, 0, 0, 0] = nt(all_left, all_right).astype(BF16)


def update_tiles(place, ranks, left, right, main, mine, other, rows, inverses):
    four = pltpu.VMEM((2, 2, 512, 128), BF16)
    shapes = (
        (512, 384), (512, 384), (512, 512), (512, 512),
        (2, 512, 256), (2, 512, 256), (2, 512, 384), (2, 2, 512, 256),
    )
    return pl.pallas_call(
        update_body,
        grid=(4,),
        out_shape=jax.ShapeDtypeStruct((2, 1, 2, 1, 512, 512), BF16),
        in_specs=[SMEM, SMEM] + [HBM] * 3 + [VMEM] * 4,
        out_specs=pl.BlockSpec(
            (1, 1, 1, 1, 512, 512), lambda s: (s // 2, 0, s % 2, 0, 0, 0)
        ),
        scratch_shapes=[four, four]
        + [pltpu.VMEM((2, 512, 512), BF16), pltpu.SemaphoreType.DMA((4,))]
        + [pltpu.VMEM(shape, BF16) for shape in shapes],
        compiler_params=params(),
        cost_estimate=cost(25 * 10**8, 8 * 2**20),
        name="update_tiles",
    )(place, ranks, *in_hbm(left, right, inverses), main, mine, other, rows)


def to_all(block, axis, size):
    sent = jnp.broadcast_to(block[None], (size,) + block.shape)
    return lax.all_to_all(sent, axis, 0, 0, tiled=True)


def per_device(left, right, ranks, pivot_inverses):
    p = lax.axis_index("row")
    q = lax.axis_index("col")
    place = jnp.stack([p, q]).astype(jnp.int32)
    ranks = ranks.reshape(2, 1, 1, 2)
    top = top_rows(ranks, left, right)
    own, near, middle, far = messages(place, ranks, left, right)
    near = lax.ppermute(near, "col", [(0, 2), (1, 15)])
    middle = lax.ppermute(middle, "col", [(0, 12), (1, 5)])
    far = lax.ppermute(far, "col", [(0, 6), (1, 11)])
    scattered = lax.all_to_all(top, "row", 0, 0, tiled=True)[:2]

    corner = jnp.where(q == 0, scattered[1], scattered[0])
    corner = to_all(jnp.concatenate([corner[0], corner[2]], axis=0), "col", N_COL)
    corner = corner.reshape(N_COL, 32, 128)[:2].reshape(64, 128)

    by_near = (q == 2) | (q == 15)
    by_middle = (q == 12) | (q == 5)
    is_head = (q < 2) | by_near | by_middle | (q == 6) | (q == 11)
    head = jnp.where(q < 2, own, jnp.where(by_near, near, jnp.where(by_middle, middle, far)))
    block = scattered.reshape(128, 128)
    sent = jnp.broadcast_to(jnp.pad(block, ((0, 64), (0, 0)))[None], (N_ROW, 192, 128))
    sent, head = lax.optimization_barrier((sent, head))
    hops = [(line[k], line[k + 1]) for line in HOLDERS for k in range(0, 8, 2)]
    moved = lax.ppermute(head[MAIN:], "col", hops)
    piece = jnp.where(is_head, head[:MAIN], moved[:MAIN])
    mine = jnp.where(is_head, head[2 * MAIN :], moved[MAIN:])
    other = lax.ppermute(mine, "col", [(i, i ^ 1) for i in range(N_COL)])

    sent = sent.at[:, 128:].set(jnp.broadcast_to(corner[None], (N_ROW, 64, 128)))
    sent, piece = lax.optimization_barrier((sent, piece))
    rows = lax.all_to_all(sent, "row", 0, 0, tiled=True).reshape(N_ROW, 12, 16, 128)
    main = lax.all_gather(piece, "col")
    return update_tiles(place, ranks, left, right, main, mine, other, rows, pivot_inverses)


def solution(mesh):
    in_specs = (
        P(None, "row", None, "col", None, None),
        P(None, "row", None, "col", None, None),
        P(None, "row", None, "col"),
        P(),
    )
    out_specs = P(None, "row", None, "col", None, None)
    return jax.shard_map(
        per_device, mesh=mesh, in_specs=in_specs, out_specs=out_specs, check_vma=False
    )
```

```python
import jax
import jax.numpy as jnp
from jax import lax
from jax.experimental import pallas as pl
from jax.experimental.pallas import tpu as pltpu
from jax.sharding import PartitionSpec as P

N_COL = 16
N_ROW = 32
PIECE = 256
MAIN = 240
REST = PIECE - MAIN
HOLDERS = ((0, 14, 2, 4, 6, 8, 12, 10), (1, 3, 5, 7, 11, 9, 15, 13))
OTHER_ONE = ((0, 1), (2, 3), (6, 7), (12, 13), (1, 0), (5, 6), (11, 10), (15, 14))
OTHER_TWO = ((0, 15), (2, 5), (6, 9), (12, 11), (1, 2), (5, 4), (11, 8), (15, 12))
VMEM = pl.BlockSpec(memory_space=pltpu.VMEM)
SMEM = pl.BlockSpec(memory_space=pltpu.SMEM)
HBM = pl.BlockSpec(memory_space=pltpu.HBM)
BF16 = jnp.bfloat16


def params():
    return pltpu.CompilerParams(vmem_limit_bytes=24 * 1024 * 1024)


def cost(flops, size):
    return pl.CostEstimate(flops=flops, bytes_accessed=size, transcendentals=0)


def tn(first, second):
    return lax.dot_general(
        first, second, (((0,), (0,)), ((), ())), preferred_element_type=jnp.float32
    )


def nn(first, second):
    return jnp.dot(first, second, preferred_element_type=jnp.float32)


def nt(first, second):
    return lax.dot_general(
        first, second, (((1,), (1,)), ((), ())), preferred_element_type=jnp.float32
    )


def mask_rank(tile, rank):
    column = lax.broadcasted_iota(jnp.int32, (1, 128), 1)
    return tile * jnp.where(column < rank, 1.0, 0.0).astype(BF16)


def in_hbm(*arrays):
    return [pltpu.with_memory_space_constraint(x, pltpu.HBM) for x in arrays]


def fetch(pairs, arrived):
    copies = [
        pltpu.make_async_copy(source, target, arrived.at[k])
        for k, (source, target) in enumerate(pairs)
    ]
    for copy in copies:
        copy.start()
    return copies


def top_body(ranks_hbm, left, right, top, panel, ranks, tiles, arrived):
    pairs = [(ranks_hbm, ranks)]
    for t in range(4):
        source = (left, right)[t // 2]
        pairs.append((source.at[0, 0, t % 2, 0], tiles.at[t]))
    pairs += [(left.at[:, 0, 0, 0], panel.at[0]), (right.at[:, 0, 0, 0], panel.at[1])]
    copies = fetch(pairs, arrived)
    copies[0].wait()
    for t in range(4):
        copies[1 + t].wait()
        top[:, t] = mask_rank(tiles[t], ranks[0, 0, 0, t % 2]).reshape(N_ROW, 16, 128)
    for copy in copies[5:]:
        copy.wait()


def top_rows(ranks, left, right):
    return pl.pallas_call(
        top_body,
        out_shape=(
            jax.ShapeDtypeStruct((N_ROW, 4, 16, 128), BF16),
            jax.ShapeDtypeStruct((2, 2, 512, 128), BF16),
        ),
        in_specs=[HBM] * 3,
        out_specs=[VMEM] * 2,
        scratch_shapes=[pltpu.SMEM((2, 1, 1, 2), jnp.int32)]
        + [pltpu.VMEM((4, 512, 128), BF16), pltpu.SemaphoreType.DMA((7,))],
        compiler_params=params(),
        cost_estimate=cost(10**6, 2**20),
        name="top_rows",
    )(*in_hbm(ranks, left, right))


def messages_body(
    place, ranks, panel, own, near, middle, far
):
    tiles = [mask_rank(panel[k, a], ranks[a, 0, 0, 0]) for k in range(2) for a in range(2)]
    at_zero = place[1] == 0
    chosen = (
        tiles[0],
        jnp.where(at_zero, tiles[1], tiles[3]),
        jnp.where(at_zero, tiles[3], tiles[1]),
        tiles[2],
    )
    for message, tile in zip((own, near, middle, far), chosen):
        message[:MAIN] = tile[:MAIN]
        message[MAIN : 2 * MAIN] = tile[PIECE : PIECE + MAIN]
        for k in range(8):
            rest = tiles[k // 2][PIECE * (k % 2) + MAIN : PIECE * (k % 2 + 1)]
            message[2 * MAIN + REST * k : 2 * MAIN + REST * (k + 1)] = rest


def messages(place, ranks, panel):
    message = jax.ShapeDtypeStruct((2 * MAIN + 8 * REST, 128), BF16)
    return pl.pallas_call(
        messages_body,
        out_shape=(message,) * 4,
        in_specs=[SMEM, SMEM, VMEM],
        out_specs=[VMEM] * 4,
        compiler_params=params(),
        cost_estimate=cost(10**6, 2**20),
        name="messages",
    )(place, ranks, panel)


def update_body(
    place, ranks, left_hbm, right_hbm, inverses_hbm, main, mine, other, rows, out,
    left, right, inverses, arrived, lowers, ups, second, wide, tall, upper, update, change,
):
    p, q = place[0], place[1]
    step = pl.program_id(0)
    a, b = step // 2, step % 2

    def row_tile(t):
        return rows[:, t].reshape(512, 128)

    @pl.when(step == 0)
    def _():
        copies = [
            pltpu.make_async_copy(inverses_hbm.at[k], inverses.at[k], arrived.at[k])
            for k in range(2)
        ]
        tiles = [
            pltpu.make_async_copy(left_hbm.at[:, 0, :, 0], left, arrived.at[2]),
            pltpu.make_async_copy(right_hbm.at[:, 0, :, 0], right, arrived.at[3]),
        ]
        for copy in copies:
            copy.start()
        ups[...] = jnp.concatenate([row_tile(0), row_tile(1), row_tile(10)], axis=1)
        for k in range(2):
            wide[:, 256 * k : 256 * k + 128] = row_tile(4 + k)
            upper[k, :, :128] = row_tile(6 + k)
            upper[k, :, 128:] = row_tile(2 + k)
        copies[0].wait()
        lowers[:, 256:] = tn(inverses[0], row_tile(9)).astype(BF16)
        for copy in tiles:
            copy.start()
        copies[1].wait()
        pivot = tn(inverses[1], row_tile(11)).astype(BF16)
        second[:, 128:256] = pivot
        second[:, 384:] = pivot
        even = q % 2 == 0
        rests = (
            jnp.where(even, mine[...], other[...]),
            jnp.where(even, other[...], mine[...]),
        )

        def column_tile(panel, tile):
            parts = []
            for k in (2 * tile, 2 * tile + 1):
                parts += [main[HOLDERS[panel][k]], rests[panel][REST * k : REST * (k + 1)]]
            return jnp.concatenate(parts, axis=0)

        raw = jnp.concatenate([column_tile(0, 2), column_tile(0, 3)], axis=1)
        lowers[:, :256] = tn(inverses[0], raw).astype(BF16)
        raw = jnp.concatenate([column_tile(1, 2), column_tile(1, 3)], axis=1)
        fresh = tn(inverses[1], raw).astype(BF16)
        second[:, :128] = fresh[:, :128]
        second[:, 256:384] = fresh[:, 128:]

        line = lax.broadcasted_iota(jnp.int32, (384, 384), 0)
        column = lax.broadcasted_iota(jnp.int32, (384, 384), 1)
        drop = ((line < 128) & (p == 0)) | ((column < 128) & (q == 0))
        product = tn(lowers[...], ups[...])
        inner = jnp.where(drop, 0.0, product).astype(BF16)
        for k in range(2):
            result = -nn(column_tile(0, k), inner[128 * k : 128 * (k + 1)])
            update[k] = result.astype(BF16)
            tall[k, :, :128] = column_tile(1, k)
            tall[k, :, 128:] = update[k, :, 256:]
        result = -nn(row_tile(8), inner[256:, :256])
        for k in range(2):
            wide[:, 256 * k + 128 : 256 * k + 256] = result[:, 128 * k : 128 * (k + 1)].astype(BF16)

        line = lax.broadcasted_iota(jnp.int32, (512, 512), 0)
        column = lax.broadcasted_iota(jnp.int32, (512, 512), 1)
        drop = ((line < 256) & (p <= 1)) | ((column < 256) & (q <= 1))
        product = tn(second[...], wide[...])
        inner = jnp.where(drop, 0.0, product).astype(BF16)
        for k in range(2):
            result = -nn(tall[k], inner[256 * k : 256 * (k + 1)])
            for j in range(2):
                change[k, j] = result[:, 256 * j : 256 * (j + 1)].astype(BF16)
        for copy in tiles:
            copy.wait()

    row = a * N_ROW + p
    col = b * N_COL + q
    rank = ranks[a, 0, 0, b]
    is_first = (col == 0) & (row > 0)
    is_second = (col == 1) & (row > 1)

    def pick(ref, width):
        return jnp.where(a == 0, ref[:, :128], ref[:, width : width + 128])

    near = jnp.where(
        is_first,
        pick(lowers, 128),
        jnp.where(is_second, pick(second, 256), mask_rank(right[a, b], rank)),
    )
    beside = jnp.where(is_second, second[:, 128:256], upper[b, :, 128:])
    done = jnp.where(b == 0, update[a, :, :128], update[a, :, 128:256])
    all_left = jnp.concatenate([mask_rank(left[a, b], rank), done, change[a, b]], axis=1)
    all_right = jnp.concatenate([near, beside, upper[b]], axis=1)
    out[0, 0, 0, 0] = nt(all_left, all_right).astype(BF16)


def update_tiles(place, ranks, left, right, main, mine, other, rows, inverses):
    four = pltpu.VMEM((2, 2, 512, 128), BF16)
    shapes = (
        (512, 384), (512, 384), (512, 512), (512, 512),
        (2, 512, 256), (2, 512, 256), (2, 512, 384), (2, 2, 512, 256),
    )
    return pl.pallas_call(
        update_body,
        grid=(4,),
        out_shape=jax.ShapeDtypeStruct((2, 1, 2, 1, 512, 512), BF16),
        in_specs=[SMEM, SMEM] + [HBM] * 3 + [VMEM] * 4,
        out_specs=pl.BlockSpec(
            (1, 1, 1, 1, 512, 512), lambda s: (s // 2, 0, s % 2, 0, 0, 0)
        ),
        scratch_shapes=[four, four]
        + [pltpu.VMEM((2, 512, 512), BF16), pltpu.SemaphoreType.DMA((4,))]
        + [pltpu.VMEM(shape, BF16) for shape in shapes],
        compiler_params=params(),
        cost_estimate=cost(25 * 10**8, 8 * 2**20),
        name="update_tiles",
    )(place, ranks, *in_hbm(left, right, inverses), main, mine, other, rows)


def to_all(block, axis, size):
    sent = jnp.broadcast_to(block[None], (size,) + block.shape)
    return lax.all_to_all(sent, axis, 0, 0, tiled=True)


def per_device(left, right, ranks, pivot_inverses):
    p = lax.axis_index("row")
    q = lax.axis_index("col")
    place = jnp.stack([p, q]).astype(jnp.int32)
    ranks = ranks.reshape(2, 1, 1, 2)
    top, panel = top_rows(ranks, left, right)
    own, near, middle, far = messages(place, ranks, panel)
    near = lax.ppermute(near, "col", [(0, 2), (1, 15)])
    middle = lax.ppermute(middle, "col", [(0, 12), (1, 5)])
    far = lax.ppermute(far, "col", [(0, 6), (1, 11)])
    scattered = lax.all_to_all(top, "row", 0, 0, tiled=True)[:2]

    corner = jnp.where(q == 0, scattered[1], scattered[0])
    corner = to_all(jnp.concatenate([corner[0], corner[2]], axis=0), "col", N_COL)
    corner = corner.reshape(N_COL, 32, 128)[:2].reshape(64, 128)

    by_near = (q == 2) | (q == 15)
    by_middle = (q == 12) | (q == 5)
    is_head = (q < 2) | by_near | by_middle | (q == 6) | (q == 11)
    head = jnp.where(q < 2, own, jnp.where(by_near, near, jnp.where(by_middle, middle, far)))
    block = scattered.reshape(128, 128)
    sent = jnp.broadcast_to(jnp.pad(block, ((0, 64), (0, 0)))[None], (N_ROW, 192, 128))
    sent, head = lax.optimization_barrier((sent, head))
    hops = [(line[k], line[k + 1]) for line in HOLDERS for k in range(0, 8, 2)]
    moved = lax.ppermute(head[MAIN:], "col", hops)
    piece = jnp.where(is_head, head[:MAIN], moved[:MAIN])
    mine = jnp.where(is_head, head[2 * MAIN :], moved[MAIN:])
    other = lax.ppermute(mine, "col", [(i, i ^ 1) for i in range(N_COL)])

    sent = sent.at[:, 128:].set(jnp.broadcast_to(corner[None], (N_ROW, 64, 128)))
    sent, piece = lax.optimization_barrier((sent, piece))
    rows = lax.all_to_all(sent, "row", 0, 0, tiled=True).reshape(N_ROW, 12, 16, 128)
    main = lax.all_gather(piece, "col")
    return update_tiles(place, ranks, left, right, main, mine, other, rows, pivot_inverses)


def solution(mesh):
    in_specs = (
        P(None, "row", None, "col", None, None),
        P(None, "row", None, "col", None, None),
        P(None, "row", None, "col"),
        P(),
    )
    out_specs = P(None, "row", None, "col", None, None)
    return jax.shard_map(
        per_device, mesh=mesh, in_specs=in_specs, out_specs=out_specs, check_vma=False
    )
```
